512 devices in a mesh: rep: 8 (over z_hi, core), fsdp: 64 (over y, z_lo, x).
Axes of the slice: x: 4, y: 8, z: 8 (z_hi: 4, z_lo: 2; z = z_hi * 2 + z_lo), core: 2. Of those that a mesh axis runs over, the one named last changes fastest.
Arguments:
- grad_terms: float32 [8, 64, 128, 4096], P('rep', 'fsdp'), may hold values from -16 to 16
- momentum: float32 [8, 128, 4096], P('rep', 'fsdp'), may hold values from -6 to 6
- positions: int32 [8, 128, 32], P(None, 'fsdp'), may hold values from 0 to 4095, as said below
Outputs:
- new_momentum: float32 [8, 128, 4096], P('rep', 'fsdp')
- update: float32 [128, 4096], P('fsdp')
The draws below stay inside these ranges and needn't reach their ends.
Inputs may be any that keep to these rules, and one draw needn't show every extreme that they name: The 32 positions of one group's span are distinct; position p is entry (p // 64, p % 64) of the span.
All inputs are finite; a program needn't handle non-finite values.
Results may differ from the reference program's by a relative error of at most 0.0029.
Values may be sent and summed in bfloat16 or wider, within the bound.
No kernel may reach another device: no remote copies, remote signals or barrier semaphores. Data moves between devices by JAX's collectives and lax.ppermute only.
A program may use at most 64 MiB of HBM per device.

```python
import math
import jax
import jax.numpy as jnp
from jax import lax

BLOCK = 64
K = 32
CP = 4096
REP = 8
MEMBERS = 64
SPANS = 128


def draw_positions(key, part):
    key = jax.random.fold_in(key, 11)
    spots = jnp.arange(CP, dtype=jnp.int32)
    scores = jax.random.randint(key, (REP, SPANS, CP), 0, 2 ** 18, dtype=jnp.int32) * CP + spots
    first = (jnp.arange(REP)[:, None, None] == 0) & (jnp.arange(SPANS)[None, :, None] == 0) & ((spots == 0) | (spots == CP - 1))[None, None, :]
    scores = jnp.where(first, 2 ** 31 - 1 - spots, scores)
    return lax.top_k(scores, K)[1].astype(jnp.int32)


def strengthened(array, own_key, source, target, blocks, factor):
    owner, partner = [(jnp.arange(array.shape[axis_at]) // (array.shape[axis_at] // blocks)).reshape([-1 if axis == axis_at else 1 for axis in range(array.ndim)]) for axis_at in (source, target)]
    chosen = jax.random.permutation(own_key, blocks)[partner]
    strong = (owner == chosen) | (owner == (partner + blocks // 2) % blocks)
    return jnp.where(strong, factor * array, array)


def block_levels(own_key, shape, shards, smallest, high):
    loudness = 1.0
    for axis_at, blocks in shards:
        steps = jax.random.uniform(jax.random.fold_in(jax.random.fold_in(own_key, 6), axis_at), (blocks,), jnp.float32, smallest / len(shards), high / len(shards))
        loudness = loudness * jnp.repeat(jnp.exp(steps), shape[axis_at] // blocks).reshape((-1,) + (1,) * (len(shape) - 1 - axis_at))
    return loudness


def gaussian(stream_key, extent, spread, bound, cuts=(), kind=jnp.bfloat16):
    values = spread * jax.random.normal(stream_key, extent, jnp.float32)
    if cuts:
        values = values * block_levels(stream_key, extent, cuts, -0.22, 0.18)
    return jnp.clip(values, -bound, bound).astype(kind)


def noise_with(own_key, shape, scale, most, split, heavy, kind=jnp.bfloat16):
    drawn = scale * jax.random.normal(own_key, shape, jnp.float32)
    if split:
        drawn = drawn * block_levels(own_key, shape, split, -0.22, 0.18)
    return jnp.clip(strengthened(drawn, jax.random.fold_in(own_key, 3), *heavy), -most, most).astype(kind)


def setup_inputs(seed: int = 0) -> dict:
    key_of = jax.random.split(jax.random.key(seed), 4)
    grad_terms = noise_with(key_of[0], (REP, MEMBERS, SPANS, CP), 1.0, 16.0, ((0, 8), (1, 64)), (1, 2, 64, 4.0), jnp.float32)
    momentum = gaussian(key_of[1], (REP, SPANS, CP), 1.0, 6.0, ((0, 8), (1, 64)), jnp.float32)
    positions = draw_positions(jax.random.fold_in(key_of[3], 71), 0)
    return {"grad_terms": grad_terms, "momentum": momentum, "positions": positions}


def cosine_matrix(side):
    freqs = jnp.arange(side, dtype=jnp.float32)
    spots = jnp.arange(side, dtype=jnp.float32)
    angles = math.pi * (2.0 * spots[None, :] + 1.0) * freqs[:, None] / (2.0 * side)
    scales = jnp.where(freqs == 0, jnp.float32(math.sqrt(1.0 / side)), jnp.float32(math.sqrt(2.0 / side)))
    return jnp.cos(angles) * scales[:, None]

def reference(grad_terms, momentum, positions):
    cosines = cosine_matrix(BLOCK)
    highest = lax.Precision.HIGHEST
    inverse_root = 1.0 / math.sqrt(MEMBERS)
    moments = []
    update = jnp.zeros((SPANS, CP), jnp.float32)
    rows_index = jnp.arange(SPANS, dtype=jnp.int32)[:, None]
    for member in range(REP):
        gradient = lax.optimization_barrier(jnp.sum(grad_terms[member], axis=0)) * inverse_root
        mixed = 0.9 * momentum[member] + gradient
        pieces = mixed.reshape(SPANS, BLOCK, BLOCK)
        spectra = jnp.einsum('kn,cnm,lm->ckl', cosines, pieces, cosines, precision=highest).reshape(SPANS, CP)
        places = positions[member].astype(jnp.int32)
        chosen = jnp.take_along_axis(spectra, places, axis=1).astype(jnp.bfloat16)
        sparse = jnp.zeros((SPANS, CP), jnp.float32).at[rows_index, places].set(chosen.astype(jnp.float32))
        sparse = sparse.reshape(SPANS, BLOCK, BLOCK)
        back = jnp.einsum('kn,ckl,lm->cnm', cosines, sparse, cosines, precision=highest).reshape(SPANS, CP)
        moments.append(mixed - back)
        update = update + back
    return (jnp.stack(moments), update)
```

```python
import functools
import math

import jax
import jax.numpy as jnp
import numpy as np
from jax import lax
from jax.experimental import pallas as pl
from jax.experimental.pallas import tpu as pltpu
from jax.sharding import PartitionSpec as P

SIDE = 64
LANES = 128
HIGHEST = lax.Precision.HIGHEST
F32 = jnp.float32


def cosine_matrix(side):
    freqs = np.arange(side, dtype=np.float64)[:, None]
    spots = np.arange(side, dtype=np.float64)[None, :]
    scales = np.where(freqs == 0, math.sqrt(1.0 / side), math.sqrt(2.0 / side))
    return np.cos(math.pi * (2.0 * spots + 1.0) * freqs / (2.0 * side)) * scales


def factors(rows, table_left, table_right):
    count = rows.shape[1]
    spots = lax.broadcasted_iota(jnp.int32, (SIDE, count), 0)
    column = lax.broadcasted_iota(jnp.int32, (1, count), 1) % LANES
    half, span = column // 64, (column // 32) % 2
    at_r = (spots == rows // SIDE).astype(F32)
    at_q = (spots == rows % SIDE).astype(F32)
    both = jnp.dot(table_left, at_r, precision=HIGHEST, preferred_element_type=F32)
    left = jnp.where(half == 0, both[:32], both[32:])
    wide = jnp.dot(table_right, at_q, precision=HIGHEST, preferred_element_type=F32)
    entry = lax.broadcasted_iota(jnp.int32, (2 * LANES, count), 0)
    fits = (entry // LANES == span) & ((entry % LANES) // 64 == half)
    right = jnp.where(fits, jnp.concatenate([wide, wide], axis=0), 0.0)
    return left, right


def side_by_side(spans):
    return jnp.concatenate([spans[:32], spans[32:]], axis=1)


def encode_kernel(inverse_root, parts_ref, momentum_ref, rows_ref, left_ref, right_ref, mixed_ref, chosen_ref):
    total = parts_ref[0]
    for member in range(1, parts_ref.shape[0]):
        total = total + parts_ref[member]
    mixed = 0.9 * momentum_ref[...] + total * inverse_root
    mixed_ref[...] = mixed
    left, right = factors(rows_ref[...], left_ref[...], right_ref[...])
    seen = jnp.dot(side_by_side(mixed), right, precision=HIGHEST, preferred_element_type=F32)
    sums = jnp.broadcast_to(jnp.sum(seen * left, axis=0, keepdims=True), (8, LANES))
    picked = (sums + pltpu.roll(sums, 64, 1)).astype(jnp.bfloat16).astype(F32)
    for group in range(chosen_ref.shape[0]):
        chosen_ref[group] = picked


def decode_kernel(mixed_ref, own_ref, all_ref, own_rows_ref, rows_ref, left_ref, right_ref, momentum_ref, update_ref):
    def decoded(kept, rows):
        left, right = factors(rows, left_ref[...], right_ref[...])
        wide = lax.dot_general(
            left * kept, right, (((1,), (1,)), ((), ())), precision=HIGHEST, preferred_element_type=F32
        )
        return jnp.concatenate([wide[:, :LANES], wide[:, LANES:]], axis=0)

    momentum_ref[...] = mixed_ref[...] - decoded(own_ref[0, :1], own_rows_ref[...])
    kept = jnp.concatenate([all_ref[group, :1] for group in range(all_ref.shape[0])], axis=1)
    update_ref[...] = decoded(kept, rows_ref[...])


def shards(grad_terms, momentum, positions):
    groups = lax.axis_size("rep")
    members = lax.axis_size("fsdp")
    inverse_root = 1.0 / math.sqrt(members)
    near = [[outer * 8 + inner for inner in range(8)] for outer in range(members // 8)]
    far = [[outer * 8 + inner for outer in range(members // 8)] for inner in range(8)]
    cosines = cosine_matrix(SIDE)
    table_left = jnp.asarray(np.concatenate([cosines[:, 0::2].T, cosines[:, 1::2].T]), F32)
    table_right = jnp.asarray(np.concatenate([cosines.T, cosines.T]), F32)

    terms = grad_terms[0, 0].astype(jnp.bfloat16).reshape(8, 8, SIDE, LANES)
    terms = lax.all_to_all(terms, "fsdp", 1, 1, axis_index_groups=near)
    partial = jnp.sum(terms.astype(F32), axis=1)
    partial = lax.all_to_all(partial, "fsdp", 0, 0, axis_index_groups=far)

    places = positions.reshape(groups, 64)
    places = jnp.concatenate([places, places], axis=1)
    own_places = lax.dynamic_slice_in_dim(places, lax.axis_index("rep"), 1, 0)

    mixed, chosen = pl.pallas_call(
        functools.partial(encode_kernel, inverse_root),
        out_shape=(
            jax.ShapeDtypeStruct((SIDE, LANES), F32),
            jax.ShapeDtypeStruct((groups, 8, LANES), F32),
        ),
        name="encode",
    )(partial, momentum.reshape(SIDE, LANES), own_places, table_left, table_right)
    everyone = lax.all_to_all(chosen, "rep", 0, 0)
    new_momentum, update = pl.pallas_call(
        decode_kernel,
        out_shape=(
            jax.ShapeDtypeStruct((SIDE, LANES), F32),
            jax.ShapeDtypeStruct((SIDE, LANES), F32),
        ),
        name="decode",
    )(mixed, chosen, everyone, own_places, places.reshape(1, groups * LANES), table_left, table_right)
    return (new_momentum.reshape(1, 2, SIDE * SIDE), update.reshape(2, SIDE * SIDE))


def solution(mesh):
    placed = (P("rep", "fsdp", None, None), P("rep", "fsdp", None), P(None, "fsdp", None))
    return jax.shard_map(
        shards,
        mesh=mesh,
        in_specs=placed,
        out_specs=(P("rep", "fsdp", None), P("fsdp", None)),
        check_vma=False,
    )
```

```python
import functools
import math

import jax
import jax.numpy as jnp
import numpy as np
from jax import lax
from jax.experimental import pallas as pl
from jax.experimental.pallas import tpu as pltpu
from jax.sharding import PartitionSpec as P

SIDE = 64
LANES = 128
HIGHEST = lax.Precision.HIGHEST
F32 = jnp.float32
ROOM = pltpu.CompilerParams(vmem_limit_bytes=16 << 20)


def cosine_matrix(side):
    freqs = np.arange(side, dtype=np.float64)[:, None]
    spots = np.arange(side, dtype=np.float64)[None, :]
    scales = np.where(freqs == 0, math.sqrt(1.0 / side), math.sqrt(2.0 / side))
    return np.cos(math.pi * (2.0 * spots + 1.0) * freqs / (2.0 * side)) * scales


def pack_kernel(terms_ref, out_ref):
    value = terms_ref[...]
    rows = jnp.stack([value[:, LANES * j : LANES * (j + 1)] for j in range(32)], axis=0)
    spans = jnp.swapaxes(rows, 0, 1).reshape(4, SIDE, LANES)
    out_ref[:, 0] = spans.astype(jnp.bfloat16)


def pack(terms):
    return pl.pallas_call(
        pack_kernel,
        grid=(16,),
        in_specs=[pl.BlockSpec((8, SIDE * SIDE), lambda i: (i, 0))],
        out_specs=pl.BlockSpec((4, 1, SIDE, LANES), lambda i: (i % 2, i // 2, 0, 0)),
        out_shape=jax.ShapeDtypeStruct((8, 8, SIDE, LANES), jnp.bfloat16),
        compiler_params=ROOM,
        name="pack",
    )(terms)


def factors_kernel(rows_ref, table_left_ref, table_right_ref, left_ref, right_ref):
    rows = rows_ref[...]
    count = rows.shape[1]
    spots = lax.broadcasted_iota(jnp.int32, (SIDE, count), 0)
    column = lax.broadcasted_iota(jnp.int32, (1, count), 1) % LANES
    half, span = column // 64, (column // 32) % 2
    at_r = (spots == rows // SIDE).astype(F32)
    at_q = (spots == rows % SIDE).astype(F32)
    both = jnp.dot(table_left_ref[...], at_r, precision=HIGHEST, preferred_element_type=F32)
    left_ref[...] = jnp.where(half == 0, both[:32], both[32:])
    wide = jnp.dot(table_right_ref[...], at_q, precision=HIGHEST, preferred_element_type=F32)
    entry = lax.broadcasted_iota(jnp.int32, (2 * LANES, count), 0)
    fits = (entry // LANES == span) & ((entry % LANES) // 64 == half)
    right_ref[...] = jnp.where(fits, jnp.concatenate([wide, wide], axis=0), 0.0)


def factors(rows):
    count = rows.shape[1]
    cosines = cosine_matrix(SIDE)
    table_left = jnp.asarray(np.concatenate([cosines[:, 0::2].T, cosines[:, 1::2].T]), F32)
    table_right = jnp.asarray(np.concatenate([cosines.T, cosines.T]), F32)
    return pl.pallas_call(
        factors_kernel,
        out_shape=(
            jax.ShapeDtypeStruct((32, count), F32),
            jax.ShapeDtypeStruct((2 * LANES, count), F32),
        ),
        compiler_params=ROOM,
        cost_estimate=pl.CostEstimate(flops=10**9, bytes_accessed=2 * 10**6, transcendentals=0),
        name="factors",
    )(rows, table_left, table_right)


def encode_kernel(inverse_root, parts_ref, momentum_ref, left_ref, right_ref, mixed_ref, kept_ref, sent_ref):
    total = parts_ref[0]
    for member in range(1, parts_ref.shape[0]):
        total = total + parts_ref[member]
    mixed = 0.9 * momentum_ref[...] + total * inverse_root
    mixed_ref[...] = mixed
    wide = jnp.concatenate([mixed[:32], mixed[32:]], axis=1)
    seen = jnp.dot(wide, right_ref[...], precision=HIGHEST, preferred_element_type=F32)
    sums = jnp.broadcast_to(jnp.sum(seen * left_ref[...], axis=0, keepdims=True), (8, LANES))
    kept = (sums + pltpu.roll(sums, 64, 1)).astype(jnp.bfloat16).astype(F32)
    kept_ref[...] = kept
    for group in range(sent_ref.shape[0]):
        sent_ref[group] = kept


def decoded(left, kept, right):
    return lax.dot_general(
        left * kept, right, (((1,), (1,)), ((), ())), precision=HIGHEST, preferred_element_type=F32
    )


def own_kernel(mixed_ref, kept_ref, left_ref, right_ref, out_ref):
    wide = decoded(left_ref[...], kept_ref[:1], right_ref[...])
    mixed = mixed_ref[...]
    left = [mixed[32 * span : 32 * (span + 1)] - wide[:, LANES * span : LANES * (span + 1)] for span in range(2)]
    for j in range(32):
        for span in range(2):
            out_ref[0, span : span + 1, LANES * j : LANES * (j + 1)] = left[span][j : j + 1]


def all_kernel(all_ref, left_ref, right_ref, out_ref):
    kept = jnp.concatenate([all_ref[group, :1] for group in range(all_ref.shape[0])], axis=1)
    wide = decoded(left_ref[...], kept, right_ref[...])
    for j in range(32):
        for span in range(2):
            out_ref[span : span + 1, LANES * j : LANES * (j + 1)] = wide[j : j + 1, LANES * span : LANES * (span + 1)]


def shards(grad_terms, momentum, positions):
    groups = lax.axis_size("rep")
    members = lax.axis_size("fsdp")
    inverse_root = 1.0 / math.sqrt(members)
    near = [[outer * 8 + inner for inner in range(8)] for outer in range(members // 8)]
    far = [[outer * 8 + inner for outer in range(members // 8)] for inner in range(8)]

    terms = lax.all_to_all(pack(grad_terms[0, 0]), "fsdp", 0, 0, axis_index_groups=near)
    partial = jnp.sum(terms.astype(F32), axis=0)
    partial = lax.all_to_all(partial, "fsdp", 0, 0, axis_index_groups=far)

    places = positions.reshape(groups, 64)
    places = jnp.concatenate([places, places], axis=1)
    left, right = factors(places.reshape(1, groups * LANES))
    start = lax.axis_index("rep") * LANES
    own_left = lax.dynamic_slice_in_dim(left, start, LANES, 1)
    own_right = lax.dynamic_slice_in_dim(right, start, LANES, 1)

    mixed, kept, sent = pl.pallas_call(
        functools.partial(encode_kernel, inverse_root),
        out_shape=(
            jax.ShapeDtypeStruct((SIDE, LANES), F32),
            jax.ShapeDtypeStruct((8, LANES), F32),
            jax.ShapeDtypeStruct((groups, 8, LANES), F32),
        ),
        compiler_params=ROOM,
        name="encode",
    )(partial, momentum.reshape(SIDE, LANES), own_left, own_right)
    everyone = lax.all_to_all(sent, "rep", 0, 0)
    new_momentum = pl.pallas_call(
        own_kernel,
        out_shape=jax.ShapeDtypeStruct((1, 2, SIDE * SIDE), F32),
        compiler_params=ROOM,
        cost_estimate=pl.CostEstimate(flops=10**8, bytes_accessed=10**6, transcendentals=0),
        name="decode_own",
    )(mixed, kept, own_left, own_right)
    update = pl.pallas_call(
        all_kernel,
        out_shape=jax.ShapeDtypeStruct((2, SIDE * SIDE), F32),
        compiler_params=ROOM,
        name="decode_all",
    )(everyone, left, right)
    return (new_momentum, update)


def solution(mesh):
    placed = (P("rep", "fsdp", None, None), P("rep", "fsdp", None), P(None, "fsdp", None))
    return jax.shard_map(
        shards,
        mesh=mesh,
        in_specs=placed,
        out_specs=(P("rep", "fsdp", None), P("fsdp", None)),
        check_vma=False,
    )
```

```python
import functools
import math

import jax
import jax.numpy as jnp
import numpy as np
from jax import lax
from jax.experimental import pallas as pl
from jax.experimental.pallas import tpu as pltpu
from jax.sharding import PartitionSpec as P

SIDE = 64
LANES = 128
NEAR = 16
FAR = 4
HIGHEST = lax.Precision.HIGHEST
F32 = jnp.float32
ROOM = pltpu.CompilerParams(vmem_limit_bytes=16 << 20)


def cosine_matrix(side):
    freqs = np.arange(side, dtype=np.float64)[:, None]
    spots = np.arange(side, dtype=np.float64)[None, :]
    scales = np.where(freqs == 0, math.sqrt(1.0 / side), math.sqrt(2.0 / side))
    return np.cos(math.pi * (2.0 * spots + 1.0) * freqs / (2.0 * side)) * scales


def pack_kernel(terms_ref, out_ref, held, packed, in_sems, out_sems):
    def fetch(i):
        return pltpu.make_async_copy(terms_ref.at[pl.ds(8 * i, 8)], held.at[i], in_sems.at[i])

    def store(i):
        where = out_ref.at[pl.ds(4 * (i % 4), 4), i // 4]
        return pltpu.make_async_copy(packed.at[i], where, out_sems.at[i])

    for i in range(16):
        fetch(i).start()

    def step(i, _):
        fetch(i).wait()
        value = held[i]
        rows = jnp.stack([value[:, LANES * j : LANES * (j + 1)] for j in range(32)], axis=0)
        packed[i] = jnp.swapaxes(rows, 0, 1).reshape(4, SIDE, LANES).astype(jnp.bfloat16)
        store(i).start()
        return 0

    lax.fori_loop(0, 16, step, 0)
    for i in range(16):
        store(i).wait()


def pack(terms):
    return pl.pallas_call(
        pack_kernel,
        in_specs=[pl.BlockSpec(memory_space=pl.ANY)],
        out_specs=pl.BlockSpec(memory_space=pl.ANY),
        out_shape=jax.ShapeDtypeStruct((NEAR, FAR, SIDE, LANES), jnp.bfloat16),
        scratch_shapes=[
            pltpu.VMEM((16, 8, SIDE * SIDE), F32),
            pltpu.VMEM((16, 4, SIDE, LANES), jnp.bfloat16),
            pltpu.SemaphoreType.DMA((16,)),
            pltpu.SemaphoreType.DMA((16,)),
        ],
        compiler_params=ROOM,
        name="pack",
    )(pltpu.with_memory_space_constraint(terms, pltpu.HBM))


def factors_kernel(rows_ref, table_ref, flat_ref, left_ref, right_ref, own_left_ref, own_right_ref):
    rows = rows_ref[...]
    count = rows.shape[1]
    spots = lax.broadcasted_iota(jnp.int32, (SIDE, count), 0)
    span = (lax.broadcasted_iota(jnp.int32, (SIDE, count), 1) // 32) % 2
    at_r = (spots == rows // SIDE).astype(F32)
    at_q = (spots == rows % SIDE).astype(F32)
    left = jnp.dot(table_ref[...], at_r, precision=HIGHEST, preferred_element_type=F32)
    flat = jnp.dot(flat_ref[...], at_q, precision=HIGHEST, preferred_element_type=F32)
    right = jnp.concatenate([jnp.where(span == 0, flat, 0.0), jnp.where(span == 1, flat, 0.0)], axis=0)
    left_ref[...] = left[:, :-LANES]
    right_ref[...] = right[:, :-LANES]
    own_left_ref[...] = left[:, -LANES:]
    own_right_ref[...] = right[:, -LANES:]


def factors(rows):
    count = rows.shape[1] - LANES
    cosines = cosine_matrix(SIDE)
    return pl.pallas_call(
        factors_kernel,
        out_shape=(
            jax.ShapeDtypeStruct((SIDE, count), F32),
            jax.ShapeDtypeStruct((2 * SIDE, count), F32),
            jax.ShapeDtypeStruct((SIDE, LANES), F32),
            jax.ShapeDtypeStruct((2 * SIDE, LANES), F32),
        ),
        compiler_params=ROOM,
        cost_estimate=pl.CostEstimate(flops=10**9, bytes_accessed=2 * 10**6, transcendentals=0),
        name="factors",
    )(rows, jnp.asarray(np.concatenate([cosines[:, 0::2].T, cosines[:, 1::2].T]), F32), jnp.asarray(cosines.T, F32))


def exchanged(first, second):
    low = lax.broadcasted_iota(jnp.int32, (32, LANES), 1) < SIDE
    return (
        jnp.where(low, first, pltpu.roll(second, SIDE, 1)),
        jnp.where(low, pltpu.roll(first, SIDE, 1), second),
    )


def encode_kernel(inverse_root, parts_ref, momentum_ref, left_ref, right_ref, mixed_ref, kept_ref, sent_ref):
    total = parts_ref[0]
    for member in range(1, parts_ref.shape[0]):
        total = total + parts_ref[member]
    mixed = 0.9 * momentum_ref[...] + total * inverse_root
    mixed_ref[...] = mixed
    halves = jnp.concatenate(exchanged(mixed[:32], mixed[32:]), axis=0)
    seen = jnp.dot(halves, right_ref[...], precision=HIGHEST, preferred_element_type=F32)
    sums = jnp.sum(seen * left_ref[...], axis=0, keepdims=True)
    kept = jnp.broadcast_to(sums, (8, LANES)).astype(jnp.bfloat16).astype(F32)
    kept_ref[...] = kept
    for group in range(sent_ref.shape[0]):
        sent_ref[group] = kept


def decoded(left, kept, right):
    wide = lax.dot_general(
        left * kept, right, (((1,), (1,)), ((), ())), precision=HIGHEST, preferred_element_type=F32
    )
    return exchanged(wide[:32], wide[32:])


def own_kernel(mixed_ref, kept_ref, left_ref, right_ref, out_ref):
    low = lax.broadcasted_iota(jnp.int32, (1, LANES), 1) < SIDE
    spans = decoded(left_ref[...], jnp.where(low, kept_ref[:1], 0.0), right_ref[...])
    for span in range(2):
        rest = mixed_ref[32 * span : 32 * (span + 1)] - spans[span]
        for j in range(32):
            out_ref[0, span : span + 1, LANES * j : LANES * (j + 1)] = rest[j : j + 1]


def all_kernel(all_ref, left_ref, right_ref, out_ref):
    low = lax.broadcasted_iota(jnp.int32, (1, LANES), 1) < SIDE
    pairs = [jnp.where(low, all_ref[i, :1], all_ref[i + 1, :1]) for i in range(0, all_ref.shape[0], 2)]
    spans = decoded(left_ref[...], jnp.concatenate(pairs, axis=1), right_ref[...])
    for span in range(2):
        for j in range(32):
            out_ref[span : span + 1, LANES * j : LANES * (j + 1)] = spans[span][j : j + 1]


def shards(grad_terms, momentum, positions):
    groups = lax.axis_size("rep")
    members = lax.axis_size("fsdp")
    inverse_root = 1.0 / math.sqrt(members)
    near = [[outer * NEAR + inner for inner in range(NEAR)] for outer in range(FAR)]
    far = [[outer * NEAR + inner for outer in range(FAR)] for inner in range(NEAR)]

    terms = lax.all_to_all(pack(grad_terms[0, 0]), "fsdp", 0, 0, axis_index_groups=near)
    partial = jnp.sum(terms.astype(F32), axis=0)
    partial = lax.all_to_all(partial, "fsdp", 0, 0, axis_index_groups=far)

    places = positions.reshape(groups, SIDE)
    own = lax.dynamic_slice_in_dim(places, lax.axis_index("rep"), 1, 0)
    left, right, own_left, own_right = factors(jnp.concatenate([places.reshape(1, groups * SIDE), own, own], axis=1))

    mixed, kept, sent = pl.pallas_call(
        functools.partial(encode_kernel, inverse_root),
        out_shape=(
            jax.ShapeDtypeStruct((SIDE, LANES), F32),
            jax.ShapeDtypeStruct((8, LANES), F32),
            jax.ShapeDtypeStruct((groups, 8, LANES), F32),
        ),
        compiler_params=ROOM,
        name="encode",
    )(partial, momentum.reshape(SIDE, LANES), own_left, own_right)
    everyone = lax.all_to_all(sent, "rep", 0, 0)
    new_momentum = pl.pallas_call(
        own_kernel,
        out_shape=jax.ShapeDtypeStruct((1, 2, SIDE * SIDE), F32),
        compiler_params=ROOM,
        cost_estimate=pl.CostEstimate(flops=10**8, bytes_accessed=10**6, transcendentals=0),
        name="decode_own",
    )(mixed, kept, own_left, own_right)
    update = pl.pallas_call(
        all_kernel,
        out_shape=jax.ShapeDtypeStruct((2, SIDE * SIDE), F32),
        compiler_params=ROOM,
        name="decode_all",
    )(everyone, left, right)
    return (new_momentum, update)


def solution(mesh):
    placed = (P("rep", "fsdp", None, None), P("rep", "fsdp", None), P(None, "fsdp", None))
    return jax.shard_map(
        shards,
        mesh=mesh,
        in_specs=placed,
        out_specs=(P("rep", "fsdp", None), P("fsdp", None)),
        check_vma=False,
    )
```

```python
import functools
import math

import jax
import jax.numpy as jnp
import numpy as np
from jax import lax
from jax.experimental import pallas as pl
from jax.experimental.pallas import tpu as pltpu
from jax.sharding import PartitionSpec as P

SIDE = 64
LANES = 128
NEAR = 16
FAR = 4
HIGHEST = lax.Precision.HIGHEST
F32 = jnp.float32
ROOM = pltpu.CompilerParams(vmem_limit_bytes=16 << 20)


def cosine_matrix(side):
    freqs = np.arange(side, dtype=np.float64)[:, None]
    spots = np.arange(side, dtype=np.float64)[None, :]
    scales = np.where(freqs == 0, math.sqrt(1.0 / side), math.sqrt(2.0 / side))
    return np.cos(math.pi * (2.0 * spots + 1.0) * freqs / (2.0 * side)) * scales


def pack_kernel(terms_ref, out_ref, held, packed, in_sems, out_sems):
    def fetch(i):
        return pltpu.make_async_copy(terms_ref.at[pl.ds(8 * i, 8)], held.at[i], in_sems.at[i])

    def store(i):
        where = out_ref.at[pl.ds(4 * (i % 4), 4), i // 4]
        return pltpu.make_async_copy(packed.at[i], where, out_sems.at[i])

    for i in range(16):
        fetch(i).start()

    def step(i, _):
        fetch(i).wait()
        value = held[i]
        rows = jnp.stack([value[:, LANES * j : LANES * (j + 1)] for j in range(32)], axis=0)
        packed[i] = jnp.swapaxes(rows, 0, 1).reshape(4, SIDE, LANES).astype(jnp.bfloat16)
        store(i).start()
        return 0

    lax.fori_loop(0, 16, step, 0)
    for i in range(16):
        store(i).wait()


def pack(terms):
    return pl.pallas_call(
        pack_kernel,
        in_specs=[pl.BlockSpec(memory_space=pl.ANY)],
        out_specs=pl.BlockSpec(memory_space=pl.ANY),
        out_shape=jax.ShapeDtypeStruct((NEAR, FAR, SIDE, LANES), jnp.bfloat16),
        scratch_shapes=[
            pltpu.VMEM((16, 8, SIDE * SIDE), F32),
            pltpu.VMEM((16, 4, SIDE, LANES), jnp.bfloat16),
            pltpu.SemaphoreType.DMA((16,)),
            pltpu.SemaphoreType.DMA((16,)),
        ],
        compiler_params=ROOM,
        name="pack",
    )(pltpu.with_memory_space_constraint(terms, pltpu.HBM))


def factors_kernel(rows_ref, table_ref, flat_ref, left_ref, right_ref, own_left_ref, own_right_ref):
    rows = rows_ref[...]
    count = rows.shape[1]
    spots = lax.broadcasted_iota(jnp.int32, (SIDE, count), 0)
    span = (lax.broadcasted_iota(jnp.int32, (SIDE, count), 1) // 32) % 2
    at_r = (spots == rows // SIDE).astype(F32)
    at_q = (spots == rows % SIDE).astype(F32)
    left = jnp.dot(table_ref[...], at_r, precision=HIGHEST, preferred_element_type=F32)
    flat = jnp.dot(flat_ref[...], at_q, precision=HIGHEST, preferred_element_type=F32)
    right = jnp.concatenate([jnp.where(span == 0, flat, 0.0), jnp.where(span == 1, flat, 0.0)], axis=0)
    left_ref[...] = left[:, :-LANES]
    right_ref[...] = right[:, :-LANES].T
    own_left_ref[...] = left[:, -LANES:]
    own_right_ref[...] = right[:, -LANES:]


def factors(rows):
    count = rows.shape[1] - LANES
    cosines = cosine_matrix(SIDE)
    return pl.pallas_call(
        factors_kernel,
        out_shape=(
            jax.ShapeDtypeStruct((SIDE, count), F32),
            jax.ShapeDtypeStruct((count, 2 * SIDE), F32),
            jax.ShapeDtypeStruct((SIDE, LANES), F32),
            jax.ShapeDtypeStruct((2 * SIDE, LANES), F32),
        ),
        compiler_params=ROOM,
        cost_estimate=pl.CostEstimate(flops=10**9, bytes_accessed=2 * 10**6, transcendentals=0),
        name="factors",
    )(rows, jnp.asarray(np.concatenate([cosines[:, 0::2].T, cosines[:, 1::2].T]), F32), jnp.asarray(cosines.T, F32))


def exchanged(first, second):
    low = lax.broadcasted_iota(jnp.int32, (32, LANES), 1) < SIDE
    return (
        jnp.where(low, first, pltpu.roll(second, SIDE, 1)),
        jnp.where(low, pltpu.roll(first, SIDE, 1), second),
    )


def add_kernel(parts_ref, *refs):
    out_ref = refs[-1]
    total = parts_ref[0].astype(F32)
    for member in range(1, parts_ref.shape[0]):
        total = total + parts_ref[member].astype(F32)
    out_ref[...] = total


def added(parts, *ready):
    return pl.pallas_call(
        add_kernel,
        in_specs=[pl.BlockSpec(memory_space=pltpu.VMEM)] + [pl.BlockSpec(memory_space=pl.ANY)] * len(ready),
        out_specs=pl.BlockSpec(memory_space=pltpu.VMEM),
        out_shape=jax.ShapeDtypeStruct(parts.shape[1:], F32),
        compiler_params=ROOM,
        name="add",
    )(parts, *ready)


def encode_kernel(inverse_root, parts_ref, momentum_ref, left_ref, right_ref, mixed_ref, kept_ref, sent_ref):
    total = parts_ref[0]
    for member in range(1, parts_ref.shape[0]):
        total = total + parts_ref[member]
    mixed = 0.9 * momentum_ref[...] + total * inverse_root
    mixed_ref[...] = mixed
    halves = jnp.concatenate(exchanged(mixed[:32], mixed[32:]), axis=0)
    seen = jnp.dot(halves, right_ref[...], precision=HIGHEST, preferred_element_type=F32)
    sums = jnp.sum(seen * left_ref[...], axis=0, keepdims=True)
    kept = jnp.broadcast_to(sums, (8, LANES)).astype(jnp.bfloat16).astype(F32)
    kept_ref[...] = kept
    for group in range(sent_ref.shape[0]):
        sent_ref[group] = kept


def decoded(left, kept, right):
    wide = lax.dot_general(
        left * kept, right, (((1,), (1,)), ((), ())), precision=HIGHEST, preferred_element_type=F32
    )
    return exchanged(wide[:32], wide[32:])


def own_kernel(mixed_ref, kept_ref, left_ref, right_ref, out_ref):
    low = lax.broadcasted_iota(jnp.int32, (1, LANES), 1) < SIDE
    spans = decoded(left_ref[...], jnp.where(low, kept_ref[:1], 0.0), right_ref[...])
    for span in range(2):
        rest = mixed_ref[32 * span : 32 * (span + 1)] - spans[span]
        for j in range(32):
            out_ref[0, span : span + 1, LANES * j : LANES * (j + 1)] = rest[j : j + 1]


def all_kernel(all_ref, left_ref, right_ref, out_ref):
    low = lax.broadcasted_iota(jnp.int32, (1, LANES), 1) < SIDE
    pairs = [jnp.where(low, all_ref[i, :1], all_ref[i + 1, :1]) for i in range(0, all_ref.shape[0], 2)]
    kept = left_ref[...] * jnp.concatenate(pairs, axis=1)
    wide = jnp.dot(kept, right_ref[...], precision=HIGHEST, preferred_element_type=F32)
    spans = exchanged(wide[:32], wide[32:])
    for span in range(2):
        for j in range(32):
            out_ref[span : span + 1, LANES * j : LANES * (j + 1)] = spans[span][j : j + 1]


def both_kernel(mixed_ref, kept_ref, own_left_ref, own_right_ref, all_ref, left_ref, right_ref, momentum_ref, update_ref):
    all_kernel(all_ref, left_ref, right_ref, update_ref)
    own_kernel(mixed_ref, kept_ref, own_left_ref, own_right_ref, momentum_ref)


def shards(grad_terms, momentum, positions):
    groups = lax.axis_size("rep")
    members = lax.axis_size("fsdp")
    inverse_root = 1.0 / math.sqrt(members)
    near = [[outer * NEAR + inner for inner in range(NEAR)] for outer in range(FAR)]
    far = [[outer * NEAR + inner for outer in range(FAR)] for inner in range(NEAR)]

    terms = lax.all_to_all(pack(grad_terms[0, 0]), "fsdp", 0, 0, axis_index_groups=near)
    places = positions.reshape(groups, SIDE)
    own = lax.dynamic_slice_in_dim(places, lax.axis_index("rep"), 1, 0)
    left, right, own_left, own_right = factors(jnp.concatenate([places.reshape(1, groups * SIDE), own, own], axis=1))

    flat = momentum.reshape(SIDE, LANES)
    partial = added(terms, own_left, flat)
    partial = lax.all_to_all(partial, "fsdp", 0, 0, axis_index_groups=far)

    mixed, kept, sent = pl.pallas_call(
        functools.partial(encode_kernel, inverse_root),
        out_shape=(
            jax.ShapeDtypeStruct((SIDE, LANES), F32),
            jax.ShapeDtypeStruct((8, LANES), F32),
            jax.ShapeDtypeStruct((groups, 8, LANES), F32),
        ),
        compiler_params=ROOM,
        name="encode",
    )(partial, flat, own_left, own_right)
    everyone = lax.all_to_all(sent, "rep", 0, 0)
    new_momentum, update = pl.pallas_call(
        both_kernel,
        out_shape=(jax.ShapeDtypeStruct((1, 2, SIDE * SIDE), F32), jax.ShapeDtypeStruct((2, SIDE * SIDE), F32)),
        compiler_params=ROOM,
        name="decode",
    )(mixed, kept, own_left, own_right, everyone, left, right)
    return (new_momentum, update)


def solution(mesh):
    placed = (P("rep", "fsdp", None, None), P("rep", "fsdp", None), P(None, "fsdp", None))
    return jax.shard_map(
        shards,
        mesh=mesh,
        in_specs=placed,
        out_specs=(P("rep", "fsdp", None), P("fsdp", None)),
        check_vma=False,
    )
```

```python
import functools
import math

import jax
import jax.numpy as jnp
import numpy as np
from jax import lax
from jax.experimental import pallas as pl
from jax.experimental.pallas import tpu as pltpu
from jax.sharding import PartitionSpec as P

SIDE = 64
LANES = 128
NEAR = 16
FAR = 4
HIGHEST = lax.Precision.HIGHEST
F32 = jnp.float32
ROOM = pltpu.CompilerParams(vmem_limit_bytes=16 << 20)


def cosine_matrix(side):
    freqs = np.arange(side, dtype=np.float64)[:, None]
    spots = np.arange(side, dtype=np.float64)[None, :]
    scales = np.where(freqs == 0, math.sqrt(1.0 / side), math.sqrt(2.0 / side))
    return np.cos(math.pi * (2.0 * spots + 1.0) * freqs / (2.0 * side)) * scales


def factors(rows, table, flat):
    count = rows.shape[1]
    spots = lax.broadcasted_iota(jnp.int32, (SIDE, count), 0)
    span = (lax.broadcasted_iota(jnp.int32, (SIDE, count), 1) // 32) % 2
    at_r = (spots == rows // SIDE).astype(F32)
    at_q = (spots == rows % SIDE).astype(F32)
    left = jnp.dot(table, at_r, precision=HIGHEST, preferred_element_type=F32)
    wide = jnp.dot(flat, at_q, precision=HIGHEST, preferred_element_type=F32)
    return left, jnp.concatenate([jnp.where(span == 0, wide, 0.0), jnp.where(span == 1, wide, 0.0)], axis=0)


def pack_kernel(
    terms_ref, places_ref, table_ref, flat_ref,
    out_ref, left_ref, right_ref, own_left_ref, own_right_ref,
    held, places, table, flat, sems, small_sems,
):
    def fetch(i):
        return pltpu.make_async_copy(terms_ref.at[pl.ds(8 * i, 8)], held.at[i], sems.at[i])

    pairs = ((places_ref, places), (table_ref, table), (flat_ref, flat))
    small = [pltpu.make_async_copy(source, target, small_sems.at[i]) for i, (source, target) in enumerate(pairs)]
    for i in range(16):
        fetch(i).start()
        if i == 3:
            for copy in small:
                copy.start()

    def step(i, _):
        fetch(i).wait()
        value = held[i]
        rows = jnp.stack([value[:, LANES * j : LANES * (j + 1)] for j in range(32)], axis=0)
        spans = jnp.swapaxes(rows, 0, 1).reshape(4, SIDE, LANES)
        out_ref[pl.ds(4 * (i % 4), 4), i // 4] = spans.astype(jnp.bfloat16)
        return 0

    lax.fori_loop(0, 6, step, 0)
    for copy in small:
        copy.wait()
    groups = places.shape[0]
    own = places[lax.axis_index("rep")]
    rows = [places[group, span : span + 1] for group in range(groups) for span in range(2)]
    rows = jnp.concatenate(rows + [own[:1], own[1:]] * 2, axis=1)
    left, right = factors(rows, table[...], flat[...])
    left_ref[...] = left[:, :-LANES]
    right_ref[...] = right[:, :-LANES].T
    own_left_ref[...] = left[:, -LANES:]
    own_right_ref[...] = right[:, -LANES:]
    lax.fori_loop(6, 16, step, 0)


def pack(terms, positions):
    groups = positions.shape[0]
    cosines = cosine_matrix(SIDE)
    shapes = ((SIDE, SIDE * groups), (SIDE * groups, LANES), (SIDE, LANES), (LANES, LANES))
    return pl.pallas_call(
        pack_kernel,
        in_specs=[pl.BlockSpec(memory_space=pl.ANY)] * 4,
        out_specs=(pl.BlockSpec(memory_space=pltpu.VMEM),) * 5,
        out_shape=(
            jax.ShapeDtypeStruct((NEAR, FAR, SIDE, LANES), jnp.bfloat16),
            *(jax.ShapeDtypeStruct(shape, F32) for shape in shapes),
        ),
        scratch_shapes=[
            pltpu.VMEM((16, 8, SIDE * SIDE), F32),
            pltpu.VMEM(positions.shape, jnp.int32),
            pltpu.VMEM((SIDE, SIDE), F32),
            pltpu.VMEM((SIDE, SIDE), F32),
            pltpu.SemaphoreType.DMA((16,)),
            pltpu.SemaphoreType.DMA((3,)),
        ],
        compiler_params=ROOM,
        name="pack",
    )(
        pltpu.with_memory_space_constraint(terms, pltpu.HBM),
        pltpu.with_memory_space_constraint(positions, pltpu.HBM),
        pltpu.with_memory_space_constraint(
            jnp.asarray(np.concatenate([cosines[:, 0::2].T, cosines[:, 1::2].T]), F32), pltpu.HBM
        ),
        pltpu.with_memory_space_constraint(jnp.asarray(cosines.T, F32), pltpu.HBM),
    )


def exchanged(first, second):
    low = lax.broadcasted_iota(jnp.int32, (32, LANES), 1) < SIDE
    return (
        jnp.where(low, first, pltpu.roll(second, SIDE, 1)),
        jnp.where(low, pltpu.roll(first, SIDE, 1), second),
    )


def add_kernel(parts_ref, *refs):
    out_ref = refs[-1]
    total = parts_ref[0].astype(F32)
    for member in range(1, parts_ref.shape[0]):
        total = total + parts_ref[member].astype(F32)
    out_ref[...] = total


def added(parts, *ready):
    return pl.pallas_call(
        add_kernel,
        in_specs=[pl.BlockSpec(memory_space=pltpu.VMEM)] + [pl.BlockSpec(memory_space=pl.ANY)] * len(ready),
        out_specs=pl.BlockSpec(memory_space=pltpu.VMEM),
        out_shape=jax.ShapeDtypeStruct(parts.shape[1:], F32),
        compiler_params=ROOM,
        name="add",
    )(parts, *ready)


def encode_kernel(inverse_root, parts_ref, momentum_ref, left_ref, right_ref, mixed_ref, kept_ref, sent_ref):
    total = parts_ref[0]
    for member in range(1, parts_ref.shape[0]):
        total = total + parts_ref[member]
    old = [momentum_ref[0, n // 32 : n // 32 + 1, LANES * (n % 32) : LANES * (n % 32 + 1)] for n in range(SIDE)]
    mixed = 0.9 * jnp.concatenate(old, axis=0) + total * inverse_root
    mixed_ref[...] = mixed
    halves = jnp.concatenate(exchanged(mixed[:32], mixed[32:]), axis=0)
    seen = jnp.dot(halves, right_ref[...], precision=HIGHEST, preferred_element_type=F32)
    sums = jnp.sum(seen * left_ref[...], axis=0, keepdims=True)
    kept = jnp.broadcast_to(sums, (8, LANES)).astype(jnp.bfloat16).astype(F32)
    kept_ref[...] = kept
    for group in range(sent_ref.shape[0]):
        sent_ref[group] = kept[:1]


def decoded(left, kept, right):
    wide = lax.dot_general(
        left * kept, right, (((1,), (1,)), ((), ())), precision=HIGHEST, preferred_element_type=F32
    )
    return exchanged(wide[:32], wide[32:])


def own_kernel(mixed_ref, kept_ref, left_ref, right_ref, out_ref):
    low = lax.broadcasted_iota(jnp.int32, (1, LANES), 1) < SIDE
    spans = decoded(left_ref[...], jnp.where(low, kept_ref[:1], 0.0), right_ref[...])
    for span in range(2):
        rest = mixed_ref[32 * span : 32 * (span + 1)] - spans[span]
        for j in range(32):
            out_ref[0, span : span + 1, LANES * j : LANES * (j + 1)] = rest[j : j + 1]


def all_kernel(all_ref, left_ref, right_ref, out_ref):
    low = lax.broadcasted_iota(jnp.int32, (1, LANES), 1) < SIDE
    pairs = [jnp.where(low, all_ref[i, :1], all_ref[i + 1, :1]) for i in range(0, all_ref.shape[0], 2)]
    kept = left_ref[...] * jnp.concatenate(pairs, axis=1)
    wide = jnp.dot(kept, right_ref[...], precision=HIGHEST, preferred_element_type=F32)
    spans = exchanged(wide[:32], wide[32:])
    for span in range(2):
        for j in range(32):
            out_ref[span : span + 1, LANES * j : LANES * (j + 1)] = spans[span][j : j + 1]


def both_kernel(mixed_ref, kept_ref, own_left_ref, own_right_ref, all_ref, left_ref, right_ref, momentum_ref, update_ref):
    all_kernel(all_ref, left_ref, right_ref, update_ref)
    own_kernel(mixed_ref, kept_ref, own_left_ref, own_right_ref, momentum_ref)


def shards(grad_terms, momentum, positions):
    groups = lax.axis_size("rep")
    members = lax.axis_size("fsdp")
    inverse_root = 1.0 / math.sqrt(members)
    near = [[outer * NEAR + inner for inner in range(NEAR)] for outer in range(FAR)]
    far = [[outer * NEAR + inner for outer in range(FAR)] for inner in range(NEAR)]

    terms, left, right, own_left, own_right = pack(grad_terms[0, 0], positions)
    terms = lax.all_to_all(terms, "fsdp", 0, 0, axis_index_groups=near)
    partial = added(terms)
    partial = lax.all_to_all(partial, "fsdp", 0, 0, axis_index_groups=far)

    mixed, kept, sent = pl.pallas_call(
        functools.partial(encode_kernel, inverse_root),
        out_shape=(
            jax.ShapeDtypeStruct((SIDE, LANES), F32),
            jax.ShapeDtypeStruct((8, LANES), F32),
            jax.ShapeDtypeStruct((groups, 1, LANES), F32),
        ),
        compiler_params=ROOM,
        name="encode",
    )(partial, momentum, own_left, own_right)
    everyone = lax.all_to_all(sent, "rep", 0, 0)
    new_momentum, update = pl.pallas_call(
        both_kernel,
        out_shape=(jax.ShapeDtypeStruct((1, 2, SIDE * SIDE), F32), jax.ShapeDtypeStruct((2, SIDE * SIDE), F32)),
        compiler_params=ROOM,
        name="decode",
    )(mixed, kept, own_left, own_right, everyone, left, right)
    return (new_momentum, update)


def solution(mesh):
    placed = (P("rep", "fsdp", None, None), P("rep", "fsdp", None), P(None, "fsdp", None))
    return jax.shard_map(
        shards,
        mesh=mesh,
        in_specs=placed,
        out_specs=(P("rep", "fsdp", None), P("fsdp", None)),
        check_vma=False,
    )
```

```python
import functools
import math

import jax
import jax.numpy as jnp
import numpy as np
from jax import lax
from jax.experimental import pallas as pl
from jax.experimental.pallas import tpu as pltpu
from jax.sharding import PartitionSpec as P

SIDE = 64
LANES = 128
NEAR = 16
FAR = 4
HIGHEST = lax.Precision.HIGHEST
F32 = jnp.float32
ROOM = pltpu.CompilerParams(vmem_limit_bytes=16 << 20)


def cosine_matrix(side):
    freqs = np.arange(side, dtype=np.float64)[:, None]
    spots = np.arange(side, dtype=np.float64)[None, :]
    scales = np.where(freqs == 0, math.sqrt(1.0 / side), math.sqrt(2.0 / side))
    return np.cos(math.pi * (2.0 * spots + 1.0) * freqs / (2.0 * side)) * scales


def factors(rows, table, flat):
    count = rows.shape[1]
    spots = lax.broadcasted_iota(jnp.int32, (SIDE, count), 0)
    span = (lax.broadcasted_iota(jnp.int32, (SIDE, count), 1) // 32) % 2
    at_r = (spots == rows // SIDE).astype(F32)
    at_q = (spots == rows % SIDE).astype(F32)
    left = jnp.dot(table, at_r, precision=HIGHEST, preferred_element_type=F32)
    wide = jnp.dot(flat, at_q, precision=HIGHEST, preferred_element_type=F32)
    return left, jnp.concatenate([jnp.where(span == 0, wide, 0.0), jnp.where(span == 1, wide, 0.0)], axis=0)


def pack_kernel(
    terms_ref, places_ref, table_ref, flat_ref,
    out_ref, left_ref, right_ref, own_left_ref, own_right_ref,
    held, places, table, flat, sems, small_sems,
):
    def fetch(i):
        return pltpu.make_async_copy(terms_ref.at[pl.ds(8 * i, 8)], held.at[i], sems.at[i])

    pairs = ((places_ref, places), (table_ref, table), (flat_ref, flat))
    small = [pltpu.make_async_copy(source, target, small_sems.at[i]) for i, (source, target) in enumerate(pairs)]
    for i in range(16):
        fetch(i).start()
        if i == 3:
            for copy in small:
                copy.start()

    def step(i, _):
        fetch(i).wait()
        value = held[i]
        rows = jnp.stack([value[:, LANES * j : LANES * (j + 1)] for j in range(32)], axis=0)
        spans = jnp.swapaxes(rows, 0, 1).reshape(4, SIDE, LANES)
        out_ref[pl.ds(4 * (i % 4), 4), i // 4] = spans.astype(jnp.bfloat16)
        return 0

    lax.fori_loop(0, 6, step, 0)
    for copy in small:
        copy.wait()
    groups = places.shape[0]
    own = places[lax.axis_index("rep")]
    rows = [places[group, span : span + 1] for group in range(groups) for span in range(2)]
    rows = jnp.concatenate(rows + [own[:1], own[1:]] * 2, axis=1)
    left, right = factors(rows, table[...], flat[...])
    left_ref[...] = left[:, :-LANES]
    right_ref[...] = right[:, :-LANES].T
    own_left_ref[...] = left[:, -LANES:]
    own_right_ref[...] = right[:, -LANES:]
    lax.fori_loop(6, 16, step, 0)


def pack(terms, positions):
    groups = positions.shape[0]
    cosines = cosine_matrix(SIDE)
    shapes = ((SIDE, SIDE * groups), (SIDE * groups, LANES), (SIDE, LANES), (LANES, LANES))
    return pl.pallas_call(
        pack_kernel,
        in_specs=[pl.BlockSpec(memory_space=pl.ANY)] * 4,
        out_specs=(pl.BlockSpec(memory_space=pltpu.VMEM),) * 5,
        out_shape=(
            jax.ShapeDtypeStruct((NEAR, FAR, SIDE, LANES), jnp.bfloat16),
            *(jax.ShapeDtypeStruct(shape, F32) for shape in shapes),
        ),
        scratch_shapes=[
            pltpu.VMEM((16, 8, SIDE * SIDE), F32),
            pltpu.VMEM(positions.shape, jnp.int32),
            pltpu.VMEM((SIDE, SIDE), F32),
            pltpu.VMEM((SIDE, SIDE), F32),
            pltpu.SemaphoreType.DMA((16,)),
            pltpu.SemaphoreType.DMA((3,)),
        ],
        compiler_params=ROOM,
        name="pack",
    )(
        pltpu.with_memory_space_constraint(terms, pltpu.HBM),
        pltpu.with_memory_space_constraint(positions, pltpu.HBM),
        pltpu.with_memory_space_constraint(
            jnp.asarray(np.concatenate([cosines[:, 0::2].T, cosines[:, 1::2].T]), F32), pltpu.HBM
        ),
        pltpu.with_memory_space_constraint(jnp.asarray(cosines.T, F32), pltpu.HBM),
    )


def exchanged(first, second):
    low = lax.broadcasted_iota(jnp.int32, (32, LANES), 1) < SIDE
    return (
        jnp.where(low, first, pltpu.roll(second, SIDE, 1)),
        jnp.where(low, pltpu.roll(first, SIDE, 1), second),
    )


def add_kernel(parts_ref, *refs):
    out_ref = refs[-1]
    total = parts_ref[0].astype(F32)
    for member in range(1, parts_ref.shape[0]):
        total = total + parts_ref[member].astype(F32)
    out_ref[...] = total


def added(parts, *ready):
    return pl.pallas_call(
        add_kernel,
        in_specs=[pl.BlockSpec(memory_space=pltpu.VMEM)] + [pl.BlockSpec(memory_space=pl.ANY)] * len(ready),
        out_specs=pl.BlockSpec(memory_space=pltpu.VMEM),
        out_shape=jax.ShapeDtypeStruct(parts.shape[1:], F32),
        compiler_params=ROOM,
        name="add",
    )(parts, *ready)


def encode_kernel(inverse_root, parts_ref, momentum_ref, left_ref, right_ref, mixed_ref, kept_ref, sent_ref):
    total = parts_ref[0]
    for member in range(1, parts_ref.shape[0]):
        total = total + parts_ref[member]
    old = [momentum_ref[0, n // 32 : n // 32 + 1, LANES * (n % 32) : LANES * (n % 32 + 1)] for n in range(SIDE)]
    mixed = 0.9 * jnp.concatenate(old, axis=0) + total * inverse_root
    mixed_ref[...] = mixed
    halves = jnp.concatenate(exchanged(mixed[:32], mixed[32:]), axis=0)
    seen = jnp.dot(halves, right_ref[...], precision=HIGHEST, preferred_element_type=F32)
    sums = jnp.sum(seen * left_ref[...], axis=0, keepdims=True)
    kept = jnp.broadcast_to(sums, (8, LANES)).astype(jnp.bfloat16).astype(F32)
    kept_ref[...] = kept
    for group in range(sent_ref.shape[0]):
        sent_ref[group] = kept[:1]


def decoded(left, kept, right):
    wide = lax.dot_general(
        left * kept, right, (((1,), (1,)), ((), ())), precision=HIGHEST, preferred_element_type=F32
    )
    return exchanged(wide[:32], wide[32:])


def own_kernel(mixed_ref, kept_ref, left_ref, right_ref, out_ref):
    low = lax.broadcasted_iota(jnp.int32, (1, LANES), 1) < SIDE
    spans = decoded(left_ref[...], jnp.where(low, kept_ref[:1], 0.0), right_ref[...])
    for span in range(2):
        rest = mixed_ref[32 * span : 32 * (span + 1)] - spans[span]
        for j in range(32):
            out_ref[0, span : span + 1, LANES * j : LANES * (j + 1)] = rest[j : j + 1]


def all_kernel(all_ref, left_ref, right_ref, out_ref):
    low = lax.broadcasted_iota(jnp.int32, (1, LANES), 1) < SIDE
    pairs = [jnp.where(low, all_ref[i, :1], all_ref[i + 1, :1]) for i in range(0, all_ref.shape[0], 2)]
    kept = left_ref[...] * jnp.concatenate(pairs, axis=1)
    wide = jnp.dot(kept, right_ref[...], precision=HIGHEST, preferred_element_type=F32)
    spans = exchanged(wide[:32], wide[32:])
    for span in range(2):
        for j in range(32):
            out_ref[span : span + 1, LANES * j : LANES * (j + 1)] = spans[span][j : j + 1]


def both_kernel(
    mixed_ref, kept_ref, own_left_ref, own_right_ref, all_ref, left_ref, right_ref,
    momentum_ref, update_ref, momentum, update, sems,
):
    own_kernel(mixed_ref, kept_ref, own_left_ref, own_right_ref, momentum)
    first = pltpu.make_async_copy(momentum, momentum_ref, sems.at[0])
    first.start()
    all_kernel(all_ref, left_ref, right_ref, update)
    second = pltpu.make_async_copy(update, update_ref, sems.at[1])
    second.start()
    first.wait()
    second.wait()


def shards(grad_terms, momentum, positions):
    groups = lax.axis_size("rep")
    members = lax.axis_size("fsdp")
    inverse_root = 1.0 / math.sqrt(members)
    near = [[outer * NEAR + inner for inner in range(NEAR)] for outer in range(FAR)]
    far = [[outer * NEAR + inner for outer in range(FAR)] for inner in range(NEAR)]

    terms, left, right, own_left, own_right = pack(grad_terms[0, 0], positions)
    terms = lax.all_to_all(terms, "fsdp", 0, 0, axis_index_groups=near)
    partial = added(terms)
    partial = lax.all_to_all(partial, "fsdp", 0, 0, axis_index_groups=far)

    mixed, kept, sent = pl.pallas_call(
        functools.partial(encode_kernel, inverse_root),
        out_shape=(
            jax.ShapeDtypeStruct((SIDE, LANES), F32),
            jax.ShapeDtypeStruct((8, LANES), F32),
            jax.ShapeDtypeStruct((groups, 1, LANES), F32),
        ),
        compiler_params=ROOM,
        name="encode",
    )(partial, momentum, own_left, own_right)
    everyone = lax.all_to_all(sent, "rep", 0, 0)
    new_momentum, update = pl.pallas_call(
        both_kernel,
        out_shape=(jax.ShapeDtypeStruct((1, 2, SIDE * SIDE), F32), jax.ShapeDtypeStruct((2, SIDE * SIDE), F32)),
        out_specs=(pl.BlockSpec(memory_space=pl.ANY),) * 2,
        scratch_shapes=[
            pltpu.VMEM((1, 2, SIDE * SIDE), F32),
            pltpu.VMEM((2, SIDE * SIDE), F32),
            pltpu.SemaphoreType.DMA((2,)),
        ],
        compiler_params=ROOM,
        name="decode",
    )(mixed, kept, own_left, own_right, everyone, left, right)
    return (new_momentum, update)


def solution(mesh):
    placed = (P("rep", "fsdp", None, None), P("rep", "fsdp", None), P(None, "fsdp", None))
    return jax.shard_map(
        shards,
        mesh=mesh,
        in_specs=placed,
        out_specs=(P("rep", "fsdp", None), P("fsdp", None)),
        check_vma=False,
    )
```
